32 devices in a mesh: px: 4 (over z), py: 8 (over y, x, core).
Axes of the slice: x: 2, y: 2, z: 4, core: 2. Of those that a mesh axis runs over, the one named last changes fastest.
Arguments:
- right_side: float32 [16, 8, 16, 128], P(None, 'px', 'py'), may hold values from -6 to 6
- colour: int32 [8, 16, 128], P('px', 'py'), may hold values from 0 to 3
- active: int32 [8, 16, 128], P('px', 'py'), may hold values 0 or 1
- stress: float32 [6, 8, 16, 128], P(None, 'px', 'py'), may hold values from -1 to 1
- conduct: float32 [8, 16, 128], P('px', 'py'), may hold values from 0.15 to 1.5
- mass: float32 [8, 16, 128], P('px', 'py'), may hold values from 0.25 to 1
- tangent_base: float32 [16, 16], replicated, may hold values from -0.25 to 0.25
- tangent_slope: float32 [6, 16, 16], replicated, may hold values from -0.04 to 0.04
Outputs:
- solution: float32 [16, 8, 16, 128], P(None, 'px', 'py')
The draws below stay inside these ranges and needn't reach their ends.
All inputs are finite; a program needn't handle non-finite values. No bound on the sum of `active` on one device may be relied on, other than what follows from the above.
Results may differ from the reference program's by a relative error of at most 0.0001.
Values sent between devices are 32-bit elements; how exact they have to be, the bound alone decides.
A program may use at most 64 MiB of HBM per device.

```python
import math
import jax
import jax.numpy as jnp
from jax import lax

BLOCK = 16
STRESS = 6
SWEEPS = 2
COLOURS = 4
NX = 8
NY = 16
NZ = 128


def with_ends(entries, rng, least, largest):
    longest = entries.shape.index(max(entries.shape))
    spots = []
    for shift in (0, 1):
        where = [jax.random.randint(jax.random.fold_in(rng, axis), (), 0, length) for axis, length in enumerate(entries.shape)]
        where[longest] = (where[longest] + shift) % entries.shape[longest]
        spots.append(tuple(where))
    return entries.at[spots[0]].set(least).at[spots[1]].set(largest)


def block_scale(stream_key, extent, pieces, least, top_value):
    def one(dim, parts):
        draws = jax.random.uniform(jax.random.fold_in(jax.random.fold_in(stream_key, 6), dim), (parts,), jnp.float32, least / len(pieces), top_value / len(pieces))
        return jnp.repeat(jnp.exp(draws), extent[dim] // parts).reshape((-1,) + (1,) * (len(extent) - dim - 1))

    factor_of = one(*pieces[0])
    for cut in pieces[1:]:
        factor_of = factor_of * one(*cut)
    return factor_of


def gaussian(own_key, shape, deviation, most, shards=(), kind=jnp.bfloat16):
    values = jax.random.normal(own_key, shape, jnp.float32) * deviation
    if len(shards) > 0:
        values = block_scale(own_key, shape, shards, -0.22, 0.18) * values
    return jnp.clip(values, min=-most, max=most).astype(kind)


def setup_inputs(seed: int = 0) -> dict:
    arg_keys = jax.random.split(jax.random.key(seed), 9)
    right_side = gaussian(arg_keys[0], (BLOCK, NX, NY, NZ), 1.0, 6.0, ((1, 4), (2, 8)), jnp.float32)
    colour = with_ends(jax.random.randint(arg_keys[1], (NX, NY, NZ), 0, COLOURS), jax.random.fold_in(arg_keys[1], 1), 0, COLOURS - 1).astype(jnp.int32)
    active = with_ends((jax.random.randint(arg_keys[2], (NX, NY, NZ), 0, 8) < 7).astype(jnp.int32), jax.random.fold_in(arg_keys[2], 1), 0, 1)
    stress = jnp.clip(jax.random.uniform(arg_keys[3], (STRESS, NX, NY, NZ), jnp.float32, -1.0, 1.0) * block_scale(arg_keys[3], (STRESS, NX, NY, NZ), ((1, 4), (2, 8)), -0.4, 0.0), -1.0, 1.0)
    conduct = jnp.clip(jnp.exp(math.log(1.5) - 2.3025851 * jax.random.uniform(arg_keys[4], (NX, NY, NZ), jnp.float32) ** block_scale(arg_keys[4], (NX, NY, NZ), ((0, 4), (1, 8)), -0.2, 0.2)), 0.15, 1.5)
    mass = jnp.clip(jnp.exp(math.log(1.0) - 1.3862944 * jax.random.uniform(arg_keys[5], (NX, NY, NZ), jnp.float32) ** block_scale(arg_keys[5], (NX, NY, NZ), ((0, 4), (1, 8)), -0.2, 0.2)), 0.25, 1.0)
    tangent_base = jnp.clip(jax.random.uniform(arg_keys[6], (BLOCK, BLOCK), jnp.float32, -0.25, 0.25), -0.25, 0.25)
    tangent_slope = jnp.clip(jax.random.uniform(arg_keys[7], (STRESS, BLOCK, BLOCK), jnp.float32, -0.04, 0.04), -0.04, 0.04)
    return {"right_side": right_side, "colour": colour, "active": active, "stress": stress, "conduct": conduct, "mass": mass, "tangent_base": tangent_base, "tangent_slope": tangent_slope}


SHIFT_DIAG = 0.25


def coupling_table():
    stiff_one = ((1.0, -1.0), (-1.0, 1.0))
    mass_one = ((1.0 / 3.0, 1.0 / 6.0), (1.0 / 6.0, 1.0 / 3.0))
    table = []
    for first in range(8):
        row_values = []
        bits_first = ((first >> 2) & 1, (first >> 1) & 1, first & 1)
        for second in range(8):
            bits_second = ((second >> 2) & 1, (second >> 1) & 1, second & 1)
            entry = 0.0
            for direction in range(3):
                term = stiff_one[bits_first[direction]][bits_second[direction]]
                for other in range(3):
                    if other != direction:
                        term = term * mass_one[bits_first[other]][bits_second[other]]
                entry = entry + term
            row_values.append(entry)
        table.append(row_values)
    return table


def corner_bits(corner):
    return (corner >> 2) & 1, (corner >> 1) & 1, corner & 1


def element_tangents(stress, tangent_base, tangent_slope):
    blocks = tangent_base.shape[0]
    identity_block = jnp.eye(blocks, dtype=jnp.float32)[:, :, None, None, None]
    varied = jnp.einsum("kpq,kxyz->pqxyz", tangent_slope, stress, precision=lax.Precision.HIGHEST)
    return identity_block + 0.125 * (tangent_base[:, :, None, None, None] + varied)


def assemble_diag(tangent, diag_weight):
    span_first, span_second, span_third = tangent.shape[2:]
    weighted = tangent * diag_weight[None, None]
    total = jnp.zeros(tangent.shape[:2] + (span_first + 1, span_second + 1, span_third + 1), jnp.float32)
    for corner in range(8):
        bit_x, bit_y, bit_z = corner_bits(corner)
        total = total.at[:, :, bit_x:bit_x + span_first, bit_y:bit_y + span_second, bit_z:bit_z + span_third].add(weighted)
    return total


def apply_elements(tangent, stiff_weight, mass_weight, values):
    span_first, span_second, span_third = tangent.shape[2:]
    corners = []
    for corner in range(8):
        bit_x, bit_y, bit_z = corner_bits(corner)
        corners.append(values[:, bit_x:bit_x + span_first, bit_y:bit_y + span_second, bit_z:bit_z + span_third])
    stacked = jnp.stack(corners, axis=1)
    products = jnp.einsum("pqxyz,qbxyz->pbxyz", tangent, stacked, precision=lax.Precision.HIGHEST)
    coupling = jnp.array(coupling_table(), dtype=jnp.float32)
    coupled = jnp.einsum("ab,pbxyz->paxyz", coupling, products, precision=lax.Precision.HIGHEST)
    element_terms = stiff_weight[None, None] * coupled + mass_weight[None, None] * products
    total = jnp.zeros(values.shape, jnp.float32)
    for corner in range(8):
        bit_x, bit_y, bit_z = corner_bits(corner)
        total = total.at[:, bit_x:bit_x + span_first, bit_y:bit_y + span_second, bit_z:bit_z + span_third].add(element_terms[:, corner])
    return total


def invert_blocks(matrices):
    order_count = matrices.shape[0]
    working = matrices
    inverse = jnp.broadcast_to(jnp.eye(order_count, dtype=jnp.float32)[:, :, None], matrices.shape)
    for pivot_index in range(order_count):
        pivots = working[pivot_index, pivot_index]
        row_working = working[pivot_index] / pivots[None]
        row_inverse = inverse[pivot_index] / pivots[None]
        factor = working[:, pivot_index]
        working = working - factor[:, None, :] * row_working[None]
        inverse = inverse - factor[:, None, :] * row_inverse[None]
        working = working.at[pivot_index].set(row_working)
        inverse = inverse.at[pivot_index].set(row_inverse)
    return inverse


def reference(right_side, colour, active, stress, conduct, mass, tangent_base, tangent_slope):
    blocks = right_side.shape[0]
    first_ids = lax.broadcasted_iota(jnp.int32, (NX, NY, NZ), 0)
    second_ids = lax.broadcasted_iota(jnp.int32, (NX, NY, NZ), 1)
    third_ids = lax.broadcasted_iota(jnp.int32, (NX, NY, NZ), 2)
    inside = (first_ids < NX - 1) & (second_ids < NY - 1) & (third_ids < NZ - 1)
    weight = active.astype(jnp.float32) * inside.astype(jnp.float32)
    tangent = element_tangents(stress, tangent_base, tangent_slope)
    stiff_weight = weight * conduct
    mass_weight = weight * mass * 0.125
    diag_weight = stiff_weight * coupling_table()[0][0] + mass_weight
    diag_total = assemble_diag(tangent, diag_weight)[:, :, :NX, :NY, :NZ]
    full = diag_total + SHIFT_DIAG * jnp.eye(blocks, dtype=jnp.float32)[:, :, None, None, None]
    inverse = invert_blocks(full.reshape(blocks, blocks, -1)).reshape(full.shape)
    solution = jnp.zeros(right_side.shape, jnp.float32)
    for sweep_index in range(SWEEPS):
        for colour_index in range(COLOURS):
            near = jnp.pad(solution, ((0, 0), (0, 1), (0, 1), (0, 1)))
            total = apply_elements(tangent, stiff_weight, mass_weight, near)[:, :NX, :NY, :NZ]
            resid = right_side - (SHIFT_DIAG * solution + total)
            update = jnp.einsum("pqxyz,qxyz->pxyz", inverse, resid, precision=lax.Precision.HIGHEST)
            solution = jnp.where(colour[None] == colour_index, solution + update, solution)
    return solution
```

```python
import functools

import jax
import jax.numpy as jnp
from jax import lax
from jax.experimental import pallas as pl
from jax.experimental.pallas import tpu as pltpu
from jax.sharding import PartitionSpec as P

SWEEPS = 2
COLOURS = 4
SHIFT_DIAG = 0.25
MESH = pl.DeviceIdType.MESH
WAYS = [(dx, dy) for dx in (-1, 0, 1) for dy in (-1, 0, 1) if (dx, dy) != (0, 0)]


def kernel(
    total_x, total_y, rhs_ref, colour_ref, active_ref, stress_ref, conduct_ref, mass_ref, base_ref, slope_ref,
    out_ref, field, elem, weights, inv, mat, coef, send_sem, recv_sem, elem_send, elem_recv,
):
    count_x, count_y = total_x // 2, total_y // 2
    me_x, me_y = lax.axis_index("px"), lax.axis_index("py")
    lanes = rhs_ref.shape[1]
    blocks = base_ref.shape[0]
    stresses = slope_ref.shape[0]
    parts = stresses + 1

    def exists(dx, dy):
        found = None
        for delta, me, count in ((dx, me_x, count_x), (dy, me_y, count_y)):
            if delta == 0:
                continue
            one = me >= 1 if delta < 0 else me <= count - 2
            found = one if found is None else found & one
        return found

    def there(dx, dy):
        return (me_x + dx, me_y + dy)

    elem[...] = jnp.zeros_like(elem)
    field[...] = jnp.zeros_like(field)
    barrier = pltpu.get_barrier_semaphore()
    for dx, dy in WAYS:
        @pl.when(exists(dx, dy))
        def _():
            pl.semaphore_signal(barrier, inc=1, device_id=there(dx, dy), device_id_type=MESH)

    third = lax.broadcasted_iota(jnp.int32, (1, lanes), 1)
    for i in range(2):
        for j in range(2):
            c = 2 * i + j
            inside = (third < lanes - 1) & (2 * me_x + i < total_x - 1) & (2 * me_y + j < total_y - 1)
            weight = jnp.where(inside, active_ref[c : c + 1, :].astype(jnp.float32), 0.0)
            elem[1 + i, 1 + j, 0:stresses, :] = stress_ref[pl.ds(c, stresses, stride=4), :]
            elem[1 + i, 1 + j, stresses : stresses + 1, :] = weight * conduct_ref[c : c + 1, :]
            elem[1 + i, 1 + j, stresses + 1 : stresses + 2, :] = weight * mass_ref[c : c + 1, :] * 0.125

    span_x = 1 + (me_x >= 1).astype(jnp.int32) + (me_x <= count_x - 2).astype(jnp.int32)
    span_y = 1 + (me_y >= 1).astype(jnp.int32) + (me_y <= count_y - 2).astype(jnp.int32)
    pl.semaphore_wait(barrier, span_x * span_y - 1)

    def elem_copy(way, target):
        dx, dy = way
        src = (2 if dx else pl.ds(1, 2), 2 if dy else pl.ds(1, 2))
        dst = (0 if dx else pl.ds(1, 2), 0 if dy else pl.ds(1, 2))
        n = dx * 2 + dy - 1
        return pltpu.make_async_remote_copy(
            src_ref=elem.at[src[0], src[1]], dst_ref=elem.at[dst[0], dst[1]],
            send_sem=elem_send.at[n], recv_sem=elem_recv.at[n], device_id=target, device_id_type=MESH,
        )

    elem_ways = ((0, 1), (1, 0), (1, 1))
    for way in elem_ways:
        @pl.when(exists(*way))
        def _():
            elem_copy(way, there(*way)).start()

    row = lax.broadcasted_iota(jnp.int32, (blocks, blocks), 0)
    col = lax.broadcasted_iota(jnp.int32, (blocks, blocks), 1)
    identity = jnp.where(row == col, 1.0, 0.0).astype(jnp.float32)
    mat[...] = jnp.zeros_like(mat)
    for s in range(parts):
        block = slope_ref[s] * 0.125 if s < stresses else identity + base_ref[...] * 0.125
        mat[:, s * blocks : (s + 1) * blocks] = block
        for q in range(blocks):
            coef[s, q] = jnp.broadcast_to(block[:, q : q + 1], (blocks, lanes))
    high = mat[...].astype(jnp.bfloat16)
    low = (mat[...] - high.astype(jnp.float32)).astype(jnp.bfloat16)
    left = jnp.concatenate(
        [jnp.concatenate([high, high], axis=1), jnp.concatenate([low, low], axis=1)], axis=0
    )

    for dx, dy in elem_ways:
        @pl.when(exists(-dx, -dy))
        def _():
            elem_copy((dx, dy), there(-dx, -dy)).wait_recv()

    line = lax.broadcasted_iota(jnp.int32, (8, lanes), 0)
    diag = {}
    for ex in range(3):
        for ey in range(3):
            part = elem[ex, ey]
            stiff = part[stresses : stresses + 1]
            mass = part[stresses + 1 : stresses + 2]
            scaled = jnp.where(line == stresses, 1.0, part)
            diag[ex, ey] = scaled * (stiff * (1.0 / 3.0) + mass)
            off = scaled * (stiff * (1.0 / 12.0))
            for z, shown in enumerate((off, pltpu.roll(off, 1, 1))):
                for s in range(parts):
                    weights[ex, ey, z, s] = jnp.broadcast_to(shown[s : s + 1], (8, lanes))

    sublane = lax.broadcasted_iota(jnp.int32, (blocks, lanes), 0)
    for i in range(2):
        for j in range(2):
            c = 2 * i + j
            total = diag[i, j] + diag[i + 1, j] + diag[i, j + 1] + diag[i + 1, j + 1]
            total = total + pltpu.roll(total, 1, 1)
            spread = [jnp.broadcast_to(total[s : s + 1], (blocks, lanes)) for s in range(parts)]
            for q in range(blocks):
                value = jnp.where(sublane == q, SHIFT_DIAG, 0.0)
                for s in range(parts):
                    value = value + coef[s, q] * spread[s]
                inv[c, q] = value

    def invert(c, carry):
        columns = [inv[c, q] for q in range(blocks)]
        for r in range(blocks):
            factor = columns[r]
            scale = 1.0 / jnp.broadcast_to(factor[r : r + 1], (8, lanes))
            scale = jnp.concatenate([scale, scale], axis=0)
            for q in range(blocks):
                if q != r:
                    ratio = jnp.broadcast_to(columns[q][r : r + 1], (blocks, lanes)) * scale
                    columns[q] = jnp.where(sublane == r, ratio, columns[q] - factor * ratio)
            columns[r] = jnp.where(sublane == r, scale, -(factor * scale))
        for q in range(blocks):
            inv[c, q] = columns[q]
        return carry

    lax.fori_loop(0, 4, invert, 0)

    def solve(c, vector):
        sums = [None, None]
        for q in range(blocks):
            term = inv[c, q] * jnp.broadcast_to(vector[q : q + 1], (blocks, lanes))
            sums[q % 2] = term if sums[q % 2] is None else sums[q % 2] + term
        return sums[0] + sums[1]

    def field_copy(slot, way, target):
        n = WAYS.index(way)
        src, dst = [], []
        for delta in way:
            src.append({-1: 1, 0: pl.ds(1, 2), 1: 2}[delta])
            dst.append({-1: 3, 0: pl.ds(1, 2), 1: 0}[delta])
        return pltpu.make_async_remote_copy(
            src_ref=field.at[slot, src[0], src[1]], dst_ref=field.at[slot, dst[0], dst[1]],
            send_sem=send_sem.at[slot, n], recv_sem=recv_sem.at[slot, n], device_id=target, device_id_type=MESH,
        )

    def send(slot):
        for way in WAYS:
            @pl.when(exists(*way))
            def _():
                field_copy(slot, way, there(*way)).start()

    for i in range(2):
        for j in range(2):
            c = 2 * i + j
            first = solve(c, rhs_ref[pl.ds(c, blocks, stride=4), :])
            hit = jnp.broadcast_to(colour_ref[c : c + 1, :], (blocks, lanes)) == 0
            field[0, 1 + i, 1 + j] = jnp.where(hit, first, 0.0)
    send(0)
    for way in elem_ways:
        @pl.when(exists(*way))
        def _():
            elem_copy(way, there(*way)).wait_send()

    steps = SWEEPS * COLOURS
    gap = jnp.zeros((128 - parts * blocks, lanes), jnp.bfloat16)

    def step(t, carry):
        old = lax.rem(t + 1, 2)
        new = lax.rem(t, 2)
        for dx, dy in WAYS:
            @pl.when(exists(-dx, -dy))
            def _():
                field_copy(old, (dx, dy), there(-dx, -dy)).wait_recv()
        shade = lax.rem(t, COLOURS)
        fresh = []
        for i in range(2):
            pair = []
            for j in range(2):
                sums = [None] * parts
                for dx in (-1, 1):
                    for dy in (-1, 1):
                        ex, ey = i + (dx > 0), j + (dy > 0)
                        corner = field[old, 1 + i + dx, 1 + j + dy]
                        cross = corner + field[old, 1 + i + dx, 1 + j] + field[old, 1 + i, 1 + j + dy]
                        for z in range(2):
                            q = corner + pltpu.roll(cross, lanes - 1 if z == 0 else 1, 1)
                            for s in range(parts):
                                w = weights[ex, ey, z, s]
                                term = jnp.concatenate([w, w], axis=0) * q
                                sums[s] = term if sums[s] is None else sums[s] + term
                tops = [x.astype(jnp.bfloat16) for x in sums]
                rest = [(x - y.astype(jnp.float32)).astype(jnp.bfloat16) for x, y in zip(sums, tops)]
                pair.append(jnp.concatenate([*tops, gap, *rest, gap], axis=0))
            made = jnp.dot(left, jnp.concatenate(pair, axis=1), preferred_element_type=jnp.float32)
            made = made[:blocks] + made[blocks:]
            for j in range(2):
                c = 2 * i + j
                vector = rhs_ref[pl.ds(c, blocks, stride=4), :] + made[:, j * lanes : (j + 1) * lanes]
                hit = jnp.broadcast_to(colour_ref[c : c + 1, :], (blocks, lanes)) == shade
                fresh.append(jnp.where(hit, solve(c, vector), field[old, 1 + i, 1 + j]))
        for way in WAYS:
            @pl.when(exists(*way))
            def _():
                field_copy(old, way, there(*way)).wait_send()
        for c in range(4):
            field[new, 1 + c // 2, 1 + c % 2] = fresh[c]
        for way in WAYS:
            @pl.when(exists(*way) & (t < steps - 1))
            def _():
                field_copy(new, way, there(*way)).start()
        return carry

    lax.fori_loop(1, steps, step, 0)
    for c in range(4):
        out_ref[pl.ds(c, blocks, stride=4), :] = field[(steps - 1) % 2, 1 + c // 2, 1 + c % 2]


def on_device(right_side, colour, active, stress, conduct, mass, tangent_base, tangent_slope):
    blocks, span_x, span_y, lanes = right_side.shape
    assert (span_x, span_y) == (2, 2)
    stresses = stress.shape[0]
    parts = stresses + 1
    total_x, total_y = span_x * lax.axis_size("px"), span_y * lax.axis_size("py")
    vmem = pl.BlockSpec(memory_space=pltpu.VMEM)
    flat = pl.pallas_call(
        functools.partial(kernel, total_x, total_y),
        out_shape=jax.ShapeDtypeStruct((blocks * 4, lanes), jnp.float32),
        in_specs=[vmem] * 8,
        out_specs=vmem,
        scratch_shapes=[
            pltpu.VMEM((2, 4, 4, blocks, lanes), jnp.float32),
            pltpu.VMEM((3, 3, stresses + 2, lanes), jnp.float32),
            pltpu.VMEM((3, 3, 2, parts, 8, lanes), jnp.float32),
            pltpu.VMEM((4, blocks, blocks, lanes), jnp.float32),
            pltpu.VMEM((blocks, 128), jnp.float32),
            pltpu.VMEM((parts, blocks, blocks, lanes), jnp.float32),
            pltpu.SemaphoreType.DMA((2, 8)),
            pltpu.SemaphoreType.DMA((2, 8)),
            pltpu.SemaphoreType.DMA((3,)),
            pltpu.SemaphoreType.DMA((3,)),
        ],
        compiler_params=pltpu.CompilerParams(
            collective_id=0, has_side_effects=True, vmem_limit_bytes=24 * 1024 * 1024
        ),
        name="gauss_seidel",
    )(
        right_side.reshape(blocks * 4, lanes),
        colour.reshape(4, lanes),
        active.reshape(4, lanes),
        stress.reshape(stresses * 4, lanes),
        conduct.reshape(4, lanes),
        mass.reshape(4, lanes),
        tangent_base,
        tangent_slope,
    )
    return flat.reshape(right_side.shape)


def solution(mesh):
    return jax.shard_map(
        on_device,
        mesh=mesh,
        in_specs=(
            P(None, "px", "py", None),
            P("px", "py", None),
            P("px", "py", None),
            P(None, "px", "py", None),
            P("px", "py", None),
            P("px", "py", None),
            P(),
            P(),
        ),
        out_specs=P(None, "px", "py", None),
        check_vma=False,
    )
```

```python
import functools

import jax
import jax.numpy as jnp
from jax import lax
from jax.experimental import pallas as pl
from jax.experimental.pallas import tpu as pltpu
from jax.sharding import PartitionSpec as P

SWEEPS = 2
COLOURS = 4
SHIFT_DIAG = 0.25
MESH = pl.DeviceIdType.MESH
WAYS = [(dx, dy) for dx in (-1, 0, 1) for dy in (-1, 0, 1) if (dx, dy) != (0, 0)]


def kernel(
    total_x, total_y, *refs
):
    given, out_ref, staged = refs[:8], refs[8], refs[9:17]
    rhs_ref, colour_ref, active_ref, stress_ref, conduct_ref, mass_ref, base_ref, slope_ref = staged
    given_sem, field, elem, weights, inv, mat, coef, send_sem, recv_sem, elem_send, elem_recv = refs[17:]
    fetches = [pltpu.make_async_copy(a, b, given_sem.at[n]) for n, (a, b) in enumerate(zip(given, staged))]
    for fetch in fetches:
        fetch.start()
    count_x, count_y = total_x // 2, total_y // 2
    me_x, me_y = lax.axis_index("px"), lax.axis_index("py")
    lanes = rhs_ref.shape[1]
    blocks = base_ref.shape[0]
    stresses = slope_ref.shape[0]
    parts = stresses + 1

    def exists(dx, dy):
        found = None
        for delta, me, count in ((dx, me_x, count_x), (dy, me_y, count_y)):
            if delta == 0:
                continue
            one = me >= 1 if delta < 0 else me <= count - 2
            found = one if found is None else found & one
        return found

    def there(dx, dy):
        return (me_x + dx, me_y + dy)

    elem[...] = jnp.zeros_like(elem)
    field[...] = jnp.zeros_like(field)
    barrier = pltpu.get_barrier_semaphore()
    for dx, dy in WAYS:
        @pl.when(exists(dx, dy))
        def _():
            pl.semaphore_signal(barrier, inc=1, device_id=there(dx, dy), device_id_type=MESH)

    for fetch in fetches:
        fetch.wait()

    third = lax.broadcasted_iota(jnp.int32, (1, lanes), 1)
    for i in range(2):
        for j in range(2):
            c = 2 * i + j
            inside = (third < lanes - 1) & (2 * me_x + i < total_x - 1) & (2 * me_y + j < total_y - 1)
            weight = jnp.where(inside, active_ref[c : c + 1, :].astype(jnp.float32), 0.0)
            elem[1 + i, 1 + j, 0:stresses, :] = stress_ref[pl.ds(c, stresses, stride=4), :]
            elem[1 + i, 1 + j, stresses : stresses + 1, :] = weight * conduct_ref[c : c + 1, :]
            elem[1 + i, 1 + j, stresses + 1 : stresses + 2, :] = weight * mass_ref[c : c + 1, :] * 0.125

    span_x = 1 + (me_x >= 1).astype(jnp.int32) + (me_x <= count_x - 2).astype(jnp.int32)
    span_y = 1 + (me_y >= 1).astype(jnp.int32) + (me_y <= count_y - 2).astype(jnp.int32)
    pl.semaphore_wait(barrier, span_x * span_y - 1)

    def elem_copy(way, target):
        dx, dy = way
        src = (2 if dx else pl.ds(1, 2), 2 if dy else pl.ds(1, 2))
        dst = (0 if dx else pl.ds(1, 2), 0 if dy else pl.ds(1, 2))
        n = dx * 2 + dy - 1
        return pltpu.make_async_remote_copy(
            src_ref=elem.at[src[0], src[1]], dst_ref=elem.at[dst[0], dst[1]],
            send_sem=elem_send.at[n], recv_sem=elem_recv.at[n], device_id=target, device_id_type=MESH,
        )

    elem_ways = ((0, 1), (1, 0), (1, 1))
    for way in elem_ways:
        @pl.when(exists(*way))
        def _():
            elem_copy(way, there(*way)).start()

    row = lax.broadcasted_iota(jnp.int32, (blocks, blocks), 0)
    col = lax.broadcasted_iota(jnp.int32, (blocks, blocks), 1)
    identity = jnp.where(row == col, 1.0, 0.0).astype(jnp.float32)
    mat[...] = jnp.zeros_like(mat)
    for s in range(parts):
        block = slope_ref[s] * 0.125 if s < stresses else identity + base_ref[...] * 0.125
        mat[:, s * blocks : (s + 1) * blocks] = block
        for q in range(blocks):
            coef[s, q] = jnp.broadcast_to(block[:, q : q + 1], (blocks, lanes))
    high = mat[...].astype(jnp.bfloat16)
    low = (mat[...] - high.astype(jnp.float32)).astype(jnp.bfloat16)
    left = jnp.concatenate(
        [jnp.concatenate([high, high], axis=1), jnp.concatenate([low, low], axis=1)], axis=0
    )

    for dx, dy in elem_ways:
        @pl.when(exists(-dx, -dy))
        def _():
            elem_copy((dx, dy), there(-dx, -dy)).wait_recv()

    line = lax.broadcasted_iota(jnp.int32, (8, lanes), 0)
    diag = {}
    for ex in range(3):
        for ey in range(3):
            part = elem[ex, ey]
            stiff = part[stresses : stresses + 1]
            mass = part[stresses + 1 : stresses + 2]
            scaled = jnp.where(line == stresses, 1.0, part)
            diag[ex, ey] = scaled * (stiff * (1.0 / 3.0) + mass)
            off = scaled * (stiff * (1.0 / 12.0))
            for z, shown in enumerate((off, pltpu.roll(off, 1, 1))):
                for s in range(parts):
                    weights[ex, ey, z, s] = jnp.broadcast_to(shown[s : s + 1], (8, lanes))

    sublane = lax.broadcasted_iota(jnp.int32, (blocks, lanes), 0)
    for i in range(2):
        for j in range(2):
            c = 2 * i + j
            total = diag[i, j] + diag[i + 1, j] + diag[i, j + 1] + diag[i + 1, j + 1]
            total = total + pltpu.roll(total, 1, 1)
            spread = [jnp.broadcast_to(total[s : s + 1], (blocks, lanes)) for s in range(parts)]
            for q in range(blocks):
                value = jnp.where(sublane == q, SHIFT_DIAG, 0.0)
                for s in range(parts):
                    value = value + coef[s, q] * spread[s]
                inv[c, q] = value

    def invert(c, carry):
        columns = [inv[c, q] for q in range(blocks)]
        for r in range(blocks):
            factor = columns[r]
            scale = 1.0 / jnp.broadcast_to(factor[r : r + 1], (8, lanes))
            scale = jnp.concatenate([scale, scale], axis=0)
            for q in range(blocks):
                if q != r:
                    ratio = jnp.broadcast_to(columns[q][r : r + 1], (blocks, lanes)) * scale
                    columns[q] = jnp.where(sublane == r, ratio, columns[q] - factor * ratio)
            columns[r] = jnp.where(sublane == r, scale, -(factor * scale))
        for q in range(blocks):
            inv[c, q] = columns[q]
        return carry

    lax.fori_loop(0, 4, invert, 0)

    def solve(c, vector):
        sums = [None, None]
        for q in range(blocks):
            term = inv[c, q] * jnp.broadcast_to(vector[q : q + 1], (blocks, lanes))
            sums[q % 2] = term if sums[q % 2] is None else sums[q % 2] + term
        return sums[0] + sums[1]

    def field_copy(slot, way, target):
        n = WAYS.index(way)
        src, dst = [], []
        for delta in way:
            src.append({-1: 1, 0: pl.ds(1, 2), 1: 2}[delta])
            dst.append({-1: 3, 0: pl.ds(1, 2), 1: 0}[delta])
        return pltpu.make_async_remote_copy(
            src_ref=field.at[slot, src[0], src[1]], dst_ref=field.at[slot, dst[0], dst[1]],
            send_sem=send_sem.at[slot, n], recv_sem=recv_sem.at[slot, n], device_id=target, device_id_type=MESH,
        )

    def send(slot):
        for way in WAYS:
            @pl.when(exists(*way))
            def _():
                field_copy(slot, way, there(*way)).start()

    for i in range(2):
        for j in range(2):
            c = 2 * i + j
            first = solve(c, rhs_ref[pl.ds(c, blocks, stride=4), :])
            hit = jnp.broadcast_to(colour_ref[c : c + 1, :], (blocks, lanes)) == 0
            field[0, 1 + i, 1 + j] = jnp.where(hit, first, 0.0)
    send(0)
    for way in elem_ways:
        @pl.when(exists(*way))
        def _():
            elem_copy(way, there(*way)).wait_send()

    steps = SWEEPS * COLOURS
    gap = jnp.zeros((128 - parts * blocks, lanes), jnp.bfloat16)

    def step(t, carry):
        old = lax.rem(t + 1, 2)
        new = lax.rem(t, 2)
        for dx, dy in WAYS:
            @pl.when(exists(-dx, -dy))
            def _():
                field_copy(old, (dx, dy), there(-dx, -dy)).wait_recv()
        shade = lax.rem(t, COLOURS)
        fresh = []
        for i in range(2):
            pair = []
            for j in range(2):
                sums = [None] * parts
                for dx in (-1, 1):
                    for dy in (-1, 1):
                        ex, ey = i + (dx > 0), j + (dy > 0)
                        corner = field[old, 1 + i + dx, 1 + j + dy]
                        cross = corner + field[old, 1 + i + dx, 1 + j] + field[old, 1 + i, 1 + j + dy]
                        for z in range(2):
                            q = corner + pltpu.roll(cross, lanes - 1 if z == 0 else 1, 1)
                            for s in range(parts):
                                w = weights[ex, ey, z, s]
                                term = jnp.concatenate([w, w], axis=0) * q
                                sums[s] = term if sums[s] is None else sums[s] + term
                tops = [x.astype(jnp.bfloat16) for x in sums]
                rest = [(x - y.astype(jnp.float32)).astype(jnp.bfloat16) for x, y in zip(sums, tops)]
                pair.append(jnp.concatenate([*tops, gap, *rest, gap], axis=0))
            made = jnp.dot(left, jnp.concatenate(pair, axis=1), preferred_element_type=jnp.float32)
            made = made[:blocks] + made[blocks:]
            for j in range(2):
                c = 2 * i + j
                vector = rhs_ref[pl.ds(c, blocks, stride=4), :] + made[:, j * lanes : (j + 1) * lanes]
                hit = jnp.broadcast_to(colour_ref[c : c + 1, :], (blocks, lanes)) == shade
                fresh.append(jnp.where(hit, solve(c, vector), field[old, 1 + i, 1 + j]))
        for way in WAYS:
            @pl.when(exists(*way))
            def _():
                field_copy(old, way, there(*way)).wait_send()
        for c in range(4):
            field[new, 1 + c // 2, 1 + c % 2] = fresh[c]
        for way in WAYS:
            @pl.when(exists(*way) & (t < steps - 1))
            def _():
                field_copy(new, way, there(*way)).start()
        return carry

    lax.fori_loop(1, steps, step, 0)
    for c in range(4):
        out_ref[pl.ds(c, blocks, stride=4), :] = field[(steps - 1) % 2, 1 + c // 2, 1 + c % 2]


def on_device(right_side, colour, active, stress, conduct, mass, tangent_base, tangent_slope):
    blocks, span_x, span_y, lanes = right_side.shape
    assert (span_x, span_y) == (2, 2)
    stresses = stress.shape[0]
    parts = stresses + 1
    total_x, total_y = span_x * lax.axis_size("px"), span_y * lax.axis_size("py")
    vmem = pl.BlockSpec(memory_space=pltpu.VMEM)
    operands = (
        right_side.reshape(blocks * 4, lanes),
        colour.reshape(4, lanes),
        active.reshape(4, lanes),
        stress.reshape(stresses * 4, lanes),
        conduct.reshape(4, lanes),
        mass.reshape(4, lanes),
        tangent_base,
        tangent_slope,
    )
    flat = pl.pallas_call(
        functools.partial(kernel, total_x, total_y),
        out_shape=jax.ShapeDtypeStruct((blocks * 4, lanes), jnp.float32),
        in_specs=[pl.BlockSpec(memory_space=pltpu.HBM)] * 8,
        out_specs=vmem,
        scratch_shapes=[
            *[pltpu.VMEM(x.shape, x.dtype) for x in operands],
            pltpu.SemaphoreType.DMA((8,)),
            pltpu.VMEM((2, 4, 4, blocks, lanes), jnp.float32),
            pltpu.VMEM((3, 3, stresses + 2, lanes), jnp.float32),
            pltpu.VMEM((3, 3, 2, parts, 8, lanes), jnp.float32),
            pltpu.VMEM((4, blocks, blocks, lanes), jnp.float32),
            pltpu.VMEM((blocks, 128), jnp.float32),
            pltpu.VMEM((parts, blocks, blocks, lanes), jnp.float32),
            pltpu.SemaphoreType.DMA((2, 8)),
            pltpu.SemaphoreType.DMA((2, 8)),
            pltpu.SemaphoreType.DMA((3,)),
            pltpu.SemaphoreType.DMA((3,)),
        ],
        compiler_params=pltpu.CompilerParams(
            collective_id=0, has_side_effects=True, vmem_limit_bytes=60 * 1024 * 1024
        ),
        name="gauss_seidel",
    )(*operands)
    return flat.reshape(right_side.shape)


def solution(mesh):
    return jax.shard_map(
        on_device,
        mesh=mesh,
        in_specs=(
            P(None, "px", "py", None),
            P("px", "py", None),
            P("px", "py", None),
            P(None, "px", "py", None),
            P("px", "py", None),
            P("px", "py", None),
            P(),
            P(),
        ),
        out_specs=P(None, "px", "py", None),
        check_vma=False,
    )
```

```python
import functools

import jax
import jax.numpy as jnp
from jax import lax
from jax.experimental import pallas as pl
from jax.experimental.pallas import tpu as pltpu
from jax.sharding import PartitionSpec as P

SWEEPS = 2
COLOURS = 4
SHIFT_DIAG = 0.25
MESH = pl.DeviceIdType.MESH
WAYS = [(dx, dy) for dx in (-1, 0, 1) for dy in (-1, 0, 1) if (dx, dy) != (0, 0)]


def kernel(total_x, total_y, *refs):
    given, out_ref, staged = refs[:8], refs[8], refs[9:17]
    rhs_ref, colour_ref, active_ref, stress_ref, conduct_ref, mass_ref, base_ref, slope_ref = staged
    given_sem, field, mid, pack, diag, weights, inv, mat, coef, send_sem, recv_sem, pack_send, pack_recv = refs[17:]
    fetches = [pltpu.make_async_copy(a, b, given_sem.at[n]) for n, (a, b) in enumerate(zip(given, staged))]
    for fetch in fetches:
        fetch.start()
    count_x, count_y = total_x // 2, total_y // 2
    me_x, me_y = lax.axis_index("px"), lax.axis_index("py")
    lanes = rhs_ref.shape[1]
    blocks = base_ref.shape[0]
    stresses = slope_ref.shape[0]
    parts = stresses + 1
    pairs = SWEEPS * COLOURS // 2

    def exists(dx, dy):
        found = None
        for delta, me, count in ((dx, me_x, count_x), (dy, me_y, count_y)):
            if delta == 0:
                continue
            one = me >= 1 if delta < 0 else me <= count - 2
            found = one if found is None else found & one
        return found

    def there(dx, dy):
        return (me_x + dx, me_y + dy)

    pack[...] = jnp.zeros_like(pack)
    field[...] = jnp.zeros_like(field)
    barrier = pltpu.get_barrier_semaphore()
    for dx, dy in WAYS:
        @pl.when(exists(dx, dy))
        def _():
            pl.semaphore_signal(barrier, inc=1, device_id=there(dx, dy), device_id_type=MESH)

    for fetch in fetches:
        fetch.wait()

    third = lax.broadcasted_iota(jnp.int32, (1, lanes), 1)
    first_stress, stiff_row = blocks, blocks + stresses
    for i in range(2):
        for j in range(2):
            c = 2 * i + j
            inside = (third < lanes - 1) & (2 * me_x + i < total_x - 1) & (2 * me_y + j < total_y - 1)
            weight = jnp.where(inside, active_ref[c : c + 1, :].astype(jnp.float32), 0.0)
            pack[2 + i, 2 + j, 0:blocks, :] = rhs_ref[pl.ds(c, blocks, stride=4), :]
            pack[2 + i, 2 + j, first_stress:stiff_row, :] = stress_ref[pl.ds(c, stresses, stride=4), :]
            pack[2 + i, 2 + j, stiff_row : stiff_row + 1, :] = weight * conduct_ref[c : c + 1, :]
            pack[2 + i, 2 + j, stiff_row + 1 : stiff_row + 2, :] = weight * mass_ref[c : c + 1, :] * 0.125
            pack[2 + i, 2 + j, stiff_row + 2 : stiff_row + 3, :] = colour_ref[c : c + 1, :].astype(jnp.float32)

    span_x = 1 + (me_x >= 1).astype(jnp.int32) + (me_x <= count_x - 2).astype(jnp.int32)
    span_y = 1 + (me_y >= 1).astype(jnp.int32) + (me_y <= count_y - 2).astype(jnp.int32)
    pl.semaphore_wait(barrier, span_x * span_y - 1)

    def pack_copy(way, target):
        n = WAYS.index(way)
        src = [pl.ds(2, 1) if delta < 0 else pl.ds(2, 2) for delta in way]
        dst = [{-1: pl.ds(4, 1), 0: pl.ds(2, 2), 1: pl.ds(0, 2)}[delta] for delta in way]
        return pltpu.make_async_remote_copy(
            src_ref=pack.at[src[0], src[1]], dst_ref=pack.at[dst[0], dst[1]],
            send_sem=pack_send.at[n], recv_sem=pack_recv.at[n], device_id=target, device_id_type=MESH,
        )

    for way in WAYS:
        @pl.when(exists(*way))
        def _():
            pack_copy(way, there(*way)).start()

    row = lax.broadcasted_iota(jnp.int32, (blocks, blocks), 0)
    col = lax.broadcasted_iota(jnp.int32, (blocks, blocks), 1)
    identity = jnp.where(row == col, 1.0, 0.0).astype(jnp.float32)
    mat[...] = jnp.zeros_like(mat)
    for s in range(parts):
        block = slope_ref[s] * 0.125 if s < stresses else identity + base_ref[...] * 0.125
        mat[:, s * blocks : (s + 1) * blocks] = block
        for q in range(blocks):
            coef[s, q] = jnp.broadcast_to(block[:, q : q + 1], (blocks, lanes))
    high = mat[...].astype(jnp.bfloat16)
    low = (mat[...] - high.astype(jnp.float32)).astype(jnp.bfloat16)
    left = jnp.concatenate(
        [jnp.concatenate([high, high], axis=1), jnp.concatenate([low, low], axis=1)], axis=0
    )

    for dx, dy in WAYS:
        @pl.when(exists(-dx, -dy))
        def _():
            pack_copy((dx, dy), there(-dx, -dy)).wait_recv()

    line = lax.broadcasted_iota(jnp.int32, (8, lanes), 0)

    def weigh(n, carry):
        ex, ey = n // 5, lax.rem(n, 5)
        part = pack[ex, ey, first_stress : first_stress + 8]
        stiff = part[stresses : stresses + 1]
        mass = part[stresses + 1 : stresses + 2]
        scaled = jnp.where(line == stresses, 1.0, part)
        diag[ex, ey] = scaled * (stiff * (1.0 / 3.0) + mass)
        off = scaled * (stiff * (1.0 / 12.0))
        for z, shown in enumerate((off, pltpu.roll(off, 1, 1))):
            for s in range(parts):
                weights[ex, ey, z, s] = jnp.broadcast_to(shown[s : s + 1], (8, lanes))
        return carry

    lax.fori_loop(0, 25, weigh, 0)

    sublane = lax.broadcasted_iota(jnp.int32, (blocks, lanes), 0)

    def matches(a, b, shade):
        shown = pack[a, b, stiff_row + 2 : stiff_row + 3]
        return jnp.broadcast_to(shown, (blocks, lanes)) == shade

    def solve(columns, vector):
        sums = [None, None]
        for q in range(blocks):
            term = columns(q) * jnp.broadcast_to(vector[q : q + 1], (blocks, lanes))
            sums[q % 2] = term if sums[q % 2] is None else sums[q % 2] + term
        return sums[0] + sums[1]

    def invert(n, carry):
        a, b = n // 4, lax.rem(n, 4)
        total = diag[a, b] + diag[a + 1, b] + diag[a, b + 1] + diag[a + 1, b + 1]
        total = total + pltpu.roll(total, 1, 1)
        spread = [jnp.broadcast_to(total[s : s + 1], (blocks, lanes)) for s in range(parts)]
        columns = []
        for q in range(blocks):
            value = jnp.where(sublane == q, SHIFT_DIAG, 0.0)
            for s in range(parts):
                value = value + coef[s, q] * spread[s]
            columns.append(value)
        for r in range(blocks):
            factor = columns[r]
            scale = 1.0 / jnp.broadcast_to(factor[r : r + 1], (8, lanes))
            scale = jnp.concatenate([scale, scale], axis=0)
            for q in range(blocks):
                if q != r:
                    ratio = jnp.broadcast_to(columns[q][r : r + 1], (blocks, lanes)) * scale
                    columns[q] = jnp.where(sublane == r, ratio, columns[q] - factor * ratio)
            columns[r] = jnp.where(sublane == r, scale, -(factor * scale))
        for q in range(blocks):
            inv[a, b, q] = columns[q]
        first = solve(lambda q: columns[q], pack[a + 1, b + 1, 0:blocks])
        mid[a + 1, b + 1] = jnp.where(matches(a + 1, b + 1, 0.0), first, 0.0)
        return carry

    lax.fori_loop(0, 16, invert, 0)

    def field_copy(slot, way, target):
        n = WAYS.index(way)
        dst = [pl.ds({-1: 4, 0: 2, 1: 0}[delta], 2) for delta in way]
        return pltpu.make_async_remote_copy(
            src_ref=field.at[slot, pl.ds(2, 2), pl.ds(2, 2)], dst_ref=field.at[slot, dst[0], dst[1]],
            send_sem=send_sem.at[slot, n], recv_sem=recv_sem.at[slot, n], device_id=target, device_id_type=MESH,
        )

    gap = jnp.zeros((128 - parts * blocks, lanes), jnp.bfloat16)

    def update(read, write, a, places, shade):
        for b0 in places:
            pair = []
            for b in (b0, b0 + 1):
                sums = [None] * parts
                for dx in (-1, 1):
                    for dy in (-1, 1):
                        ex, ey = a if dx > 0 else a - 1, b if dy > 0 else b - 1
                        corner = read(a + dx, b + dy)
                        cross = corner + read(a + dx, b) + read(a, b + dy)
                        for z in range(2):
                            q = corner + pltpu.roll(cross, lanes - 1 if z == 0 else 1, 1)
                            for s in range(parts):
                                w = weights[ex, ey, z, s]
                                term = jnp.concatenate([w, w], axis=0) * q
                                sums[s] = term if sums[s] is None else sums[s] + term
                tops = [x.astype(jnp.bfloat16) for x in sums]
                rest = [(x - y.astype(jnp.float32)).astype(jnp.bfloat16) for x, y in zip(sums, tops)]
                pair.append(jnp.concatenate([*tops, gap, *rest, gap], axis=0))
            made = jnp.dot(left, jnp.concatenate(pair, axis=1), preferred_element_type=jnp.float32)
            made = made[:blocks] + made[blocks:]
            for k in range(2):
                b = b0 + k
                vector = pack[a, b, 0:blocks] + made[:, k * lanes : (k + 1) * lanes]
                value = solve(lambda q: inv[a - 1, b - 1, q], vector)
                write(a, b, jnp.where(matches(a, b, shade), value, read(a, b)))

    def pair_of_steps(p, carry):
        @pl.when(p > 0)
        def _():
            for dx, dy in WAYS:
                @pl.when(exists(-dx, -dy))
                def _():
                    field_copy(p - 1, (dx, dy), there(-dx, -dy)).wait_recv()

            def wide(a, inner):
                def write(x, y, value):
                    mid[x, y] = value

                shade = lax.rem(2 * p, COLOURS).astype(jnp.float32)
                update(lambda x, y: field[p - 1, x, y], write, a, (1, 3), shade)
                return inner

            lax.fori_loop(1, 5, wide, 0)

        def write(x, y, value):
            field[p, x, y] = value

        shade = lax.rem(2 * p + 1, COLOURS).astype(jnp.float32)
        for a in (2, 3):
            update(lambda x, y: mid[x, y], write, a, (2,), shade)
        for way in WAYS:
            @pl.when(exists(*way) & (p < pairs - 1))
            def _():
                field_copy(p, way, there(*way)).start()
        return carry

    lax.fori_loop(0, pairs, pair_of_steps, 0)
    for c in range(4):
        out_ref[pl.ds(c, blocks, stride=4), :] = field[pairs - 1, 2 + c // 2, 2 + c % 2]
    for way in WAYS:
        @pl.when(exists(*way))
        def _():
            pack_copy(way, there(*way)).wait_send()
            for p in range(pairs - 1):
                field_copy(p, way, there(*way)).wait_send()


def on_device(right_side, colour, active, stress, conduct, mass, tangent_base, tangent_slope):
    blocks, span_x, span_y, lanes = right_side.shape
    assert (span_x, span_y) == (2, 2)
    stresses = stress.shape[0]
    parts = stresses + 1
    pairs = SWEEPS * COLOURS // 2
    total_x, total_y = span_x * lax.axis_size("px"), span_y * lax.axis_size("py")
    vmem = pl.BlockSpec(memory_space=pltpu.VMEM)
    operands = (
        right_side.reshape(blocks * 4, lanes),
        colour.reshape(4, lanes),
        active.reshape(4, lanes),
        stress.reshape(stresses * 4, lanes),
        conduct.reshape(4, lanes),
        mass.reshape(4, lanes),
        tangent_base,
        tangent_slope,
    )
    flat = pl.pallas_call(
        functools.partial(kernel, total_x, total_y),
        out_shape=jax.ShapeDtypeStruct((blocks * 4, lanes), jnp.float32),
        in_specs=[pl.BlockSpec(memory_space=pltpu.HBM)] * 8,
        out_specs=vmem,
        scratch_shapes=[
            *[pltpu.VMEM(x.shape, x.dtype) for x in operands],
            pltpu.SemaphoreType.DMA((8,)),
            pltpu.VMEM((pairs, 6, 6, blocks, lanes), jnp.float32),
            pltpu.VMEM((6, 6, blocks, lanes), jnp.float32),
            pltpu.VMEM((6, 6, 32, lanes), jnp.float32),
            pltpu.VMEM((5, 5, 8, lanes), jnp.float32),
            pltpu.VMEM((5, 5, 2, parts, 8, lanes), jnp.float32),
            pltpu.VMEM((4, 4, blocks, blocks, lanes), jnp.float32),
            pltpu.VMEM((blocks, 128), jnp.float32),
            pltpu.VMEM((parts, blocks, blocks, lanes), jnp.float32),
            pltpu.SemaphoreType.DMA((pairs - 1, 8)),
            pltpu.SemaphoreType.DMA((pairs - 1, 8)),
            pltpu.SemaphoreType.DMA((8,)),
            pltpu.SemaphoreType.DMA((8,)),
        ],
        compiler_params=pltpu.CompilerParams(
            collective_id=0, has_side_effects=True, vmem_limit_bytes=60 * 1024 * 1024
        ),
        name="gauss_seidel",
    )(*operands)
    return flat.reshape(right_side.shape)


def solution(mesh):
    return jax.shard_map(
        on_device,
        mesh=mesh,
        in_specs=(
            P(None, "px", "py", None),
            P("px", "py", None),
            P("px", "py", None),
            P(None, "px", "py", None),
            P("px", "py", None),
            P("px", "py", None),
            P(),
            P(),
        ),
        out_specs=P(None, "px", "py", None),
        check_vma=False,
    )
```

```python
import functools

import jax
import jax.numpy as jnp
from jax import lax
from jax.experimental import pallas as pl
from jax.experimental.pallas import tpu as pltpu
from jax.sharding import PartitionSpec as P

SWEEPS = 2
COLOURS = 4
SHIFT_DIAG = 0.25
MESH = pl.DeviceIdType.MESH
SIDES = [(-1, 0), (1, 0), (0, -1), (0, 1)]
CORNERS = [(-1, -1), (-1, 1), (1, -1), (1, 1)]
WAYS = CORNERS + SIDES


def kernel(
    total_x, total_y, *refs
):
    given, out_ref, staged = refs[:8], refs[8], refs[9:17]
    rhs_ref, colour_ref, active_ref, stress_ref, conduct_ref, mass_ref, base_ref, slope_ref = staged
    given_sem, field, elem, weights, inv, mat, coef, send_sem, recv_sem, elem_send, elem_recv = refs[17:]
    fetches = [pltpu.make_async_copy(a, b, given_sem.at[n]) for n, (a, b) in enumerate(zip(given, staged))]
    for fetch in fetches:
        fetch.start()
    count_x, count_y = total_x // 2, total_y // 2
    me_x, me_y = lax.axis_index("px"), lax.axis_index("py")
    lanes = rhs_ref.shape[1]
    blocks = base_ref.shape[0]
    stresses = slope_ref.shape[0]
    parts = stresses + 1

    def exists(dx, dy):
        found = None
        for delta, me, count in ((dx, me_x, count_x), (dy, me_y, count_y)):
            if delta == 0:
                continue
            one = me >= 1 if delta < 0 else me <= count - 2
            found = one if found is None else found & one
        return found

    def there(dx, dy):
        return (me_x + dx, me_y + dy)

    elem[...] = jnp.zeros_like(elem)
    field[...] = jnp.zeros_like(field)
    barrier = pltpu.get_barrier_semaphore()
    for dx, dy in WAYS:
        @pl.when(exists(dx, dy))
        def _():
            pl.semaphore_signal(barrier, inc=1, device_id=there(dx, dy), device_id_type=MESH)

    for fetch in fetches:
        fetch.wait()

    third = lax.broadcasted_iota(jnp.int32, (1, lanes), 1)
    for i in range(2):
        for j in range(2):
            c = 2 * i + j
            inside = (third < lanes - 1) & (2 * me_x + i < total_x - 1) & (2 * me_y + j < total_y - 1)
            weight = jnp.where(inside, active_ref[c : c + 1, :].astype(jnp.float32), 0.0)
            elem[1 + i, 1 + j, 0:stresses, :] = stress_ref[pl.ds(c, stresses, stride=4), :]
            elem[1 + i, 1 + j, stresses : stresses + 1, :] = weight * conduct_ref[c : c + 1, :]
            elem[1 + i, 1 + j, stresses + 1 : stresses + 2, :] = weight * mass_ref[c : c + 1, :] * 0.125

    span_x = 1 + (me_x >= 1).astype(jnp.int32) + (me_x <= count_x - 2).astype(jnp.int32)
    span_y = 1 + (me_y >= 1).astype(jnp.int32) + (me_y <= count_y - 2).astype(jnp.int32)
    pl.semaphore_wait(barrier, span_x * span_y - 1)

    def elem_copy(way, target):
        dx, dy = way
        src = (2 if dx else pl.ds(1, 2), 2 if dy else pl.ds(1, 2))
        dst = (0 if dx else pl.ds(1, 2), 0 if dy else pl.ds(1, 2))
        n = dx * 2 + dy - 1
        return pltpu.make_async_remote_copy(
            src_ref=elem.at[src[0], src[1]], dst_ref=elem.at[dst[0], dst[1]],
            send_sem=elem_send.at[n], recv_sem=elem_recv.at[n], device_id=target, device_id_type=MESH,
        )

    elem_ways = ((0, 1), (1, 0), (1, 1))
    for way in elem_ways:
        @pl.when(exists(*way))
        def _():
            elem_copy(way, there(*way)).start()

    row = lax.broadcasted_iota(jnp.int32, (blocks, blocks), 0)
    col = lax.broadcasted_iota(jnp.int32, (blocks, blocks), 1)
    identity = jnp.where(row == col, 1.0, 0.0).astype(jnp.float32)
    mat[...] = jnp.zeros_like(mat)
    for s in range(parts):
        block = slope_ref[s] * 0.125 if s < stresses else identity + base_ref[...] * 0.125
        mat[:, s * blocks : (s + 1) * blocks] = block
        for q in range(blocks):
            coef[s, q] = jnp.broadcast_to(block[:, q : q + 1], (blocks, lanes))
    high = mat[...].astype(jnp.bfloat16)
    low = (mat[...] - high.astype(jnp.float32)).astype(jnp.bfloat16)
    left = jnp.concatenate(
        [jnp.concatenate([high, high], axis=1), jnp.concatenate([low, low], axis=1)], axis=0
    )

    for dx, dy in elem_ways:
        @pl.when(exists(-dx, -dy))
        def _():
            elem_copy((dx, dy), there(-dx, -dy)).wait_recv()

    line = lax.broadcasted_iota(jnp.int32, (8, lanes), 0)
    diag = {}
    for ex in range(3):
        for ey in range(3):
            part = elem[ex, ey]
            stiff = part[stresses : stresses + 1]
            mass = part[stresses + 1 : stresses + 2]
            scaled = jnp.where(line == stresses, 1.0, part)
            diag[ex, ey] = scaled * (stiff * (1.0 / 3.0) + mass)
            off = scaled * (stiff * (1.0 / 12.0))
            for z, shown in enumerate((off, pltpu.roll(off, 1, 1))):
                for s in range(parts):
                    weights[ex, ey, z, s] = jnp.broadcast_to(shown[s : s + 1], (8, lanes))

    sublane = lax.broadcasted_iota(jnp.int32, (blocks, lanes), 0)
    for i in range(2):
        for j in range(2):
            c = 2 * i + j
            total = diag[i, j] + diag[i + 1, j] + diag[i, j + 1] + diag[i + 1, j + 1]
            total = total + pltpu.roll(total, 1, 1)
            spread = [jnp.broadcast_to(total[s : s + 1], (blocks, lanes)) for s in range(parts)]
            for q in range(blocks):
                value = jnp.where(sublane == q, SHIFT_DIAG, 0.0)
                for s in range(parts):
                    value = value + coef[s, q] * spread[s]
                inv[c, q] = value

    def invert(c, carry):
        columns = [inv[c, q] for q in range(blocks)]
        for r in range(blocks):
            factor = columns[r]
            scale = 1.0 / jnp.broadcast_to(factor[r : r + 1], (8, lanes))
            scale = jnp.concatenate([scale, scale], axis=0)
            for q in range(blocks):
                if q != r:
                    ratio = jnp.broadcast_to(columns[q][r : r + 1], (blocks, lanes)) * scale
                    columns[q] = jnp.where(sublane == r, ratio, columns[q] - factor * ratio)
            columns[r] = jnp.where(sublane == r, scale, -(factor * scale))
        for q in range(blocks):
            inv[c, q] = columns[q]
        return carry

    lax.fori_loop(0, 4, invert, 0)

    def solve(c, vector):
        sums = [None, None]
        for q in range(blocks):
            term = inv[c, q] * jnp.broadcast_to(vector[q : q + 1], (blocks, lanes))
            sums[q % 2] = term if sums[q % 2] is None else sums[q % 2] + term
        return sums[0] + sums[1]

    def field_copy(slot, way, target):
        n = WAYS.index(way)
        src, dst = [], []
        for delta in way:
            src.append({-1: 1, 0: pl.ds(1, 2), 1: 2}[delta])
            dst.append({-1: 3, 0: pl.ds(1, 2), 1: 0}[delta])
        return pltpu.make_async_remote_copy(
            src_ref=field.at[slot, src[0], src[1]], dst_ref=field.at[slot, dst[0], dst[1]],
            send_sem=send_sem.at[slot, n], recv_sem=recv_sem.at[slot, n], device_id=target, device_id_type=MESH,
        )

    def send(slot):
        for way in WAYS:
            @pl.when(exists(*way))
            def _():
                field_copy(slot, way, there(*way)).start()

    for i in range(2):
        for j in range(2):
            c = 2 * i + j
            first = solve(c, rhs_ref[pl.ds(c, blocks, stride=4), :])
            hit = jnp.broadcast_to(colour_ref[c : c + 1, :], (blocks, lanes)) == 0
            field[0, 1 + i, 1 + j] = jnp.where(hit, first, 0.0)
    send(0)
    for way in elem_ways:
        @pl.when(exists(*way))
        def _():
            elem_copy(way, there(*way)).wait_send()

    steps = SWEEPS * COLOURS
    gap = jnp.zeros((128 - parts * blocks, lanes), jnp.bfloat16)

    def step(t, carry):
        old, new = t - 1, t
        shade = lax.rem(t, COLOURS)
        sums = [[None] * parts for _ in range(4)]

        def receive(ways):
            for dx, dy in ways:
                @pl.when(exists(-dx, -dy))
                def _():
                    field_copy(old, (dx, dy), there(-dx, -dy)).wait_recv()

        def gather(outward):
            for c in range(4):
                i, j = c // 2, c % 2
                for dx in (-1, 1):
                    for dy in (-1, 1):
                        if (dx != 1 - 2 * i) + (dy != 1 - 2 * j) != outward:
                            continue
                        ex, ey = i + (dx > 0), j + (dy > 0)
                        corner = field[old, 1 + i + dx, 1 + j + dy]
                        cross = corner + field[old, 1 + i + dx, 1 + j] + field[old, 1 + i, 1 + j + dy]
                        for z in range(2):
                            q = corner + pltpu.roll(cross, lanes - 1 if z == 0 else 1, 1)
                            for s in range(parts):
                                w = weights[ex, ey, z, s]
                                term = jnp.concatenate([w, w], axis=0) * q
                                sums[c][s] = term if sums[c][s] is None else sums[c][s] + term

        gather(0)
        receive(SIDES)
        gather(1)
        receive(CORNERS)
        gather(2)
        fresh = []
        for i in range(2):
            pair = []
            for j in range(2):
                tops = [x.astype(jnp.bfloat16) for x in sums[2 * i + j]]
                rest = [(x - y.astype(jnp.float32)).astype(jnp.bfloat16) for x, y in zip(sums[2 * i + j], tops)]
                pair.append(jnp.concatenate([*tops, gap, *rest, gap], axis=0))
            made = jnp.dot(left, jnp.concatenate(pair, axis=1), preferred_element_type=jnp.float32)
            made = made[:blocks] + made[blocks:]
            for j in range(2):
                c = 2 * i + j
                vector = rhs_ref[pl.ds(c, blocks, stride=4), :] + made[:, j * lanes : (j + 1) * lanes]
                hit = jnp.broadcast_to(colour_ref[c : c + 1, :], (blocks, lanes)) == shade
                fresh.append(jnp.where(hit, solve(c, vector), field[old, 1 + i, 1 + j]))
        for c in range(4):
            field[new, 1 + c // 2, 1 + c % 2] = fresh[c]
        for way in WAYS:
            @pl.when(exists(*way) & (t < steps - 1))
            def _():
                field_copy(new, way, there(*way)).start()
        return carry

    lax.fori_loop(1, steps, step, 0)
    for c in range(4):
        out_ref[pl.ds(c, blocks, stride=4), :] = field[steps - 1, 1 + c // 2, 1 + c % 2]

    def finish(t, carry):
        for way in WAYS:
            @pl.when(exists(*way))
            def _():
                field_copy(t, way, there(*way)).wait_send()
        return carry

    lax.fori_loop(0, steps - 1, finish, 0)


def on_device(right_side, colour, active, stress, conduct, mass, tangent_base, tangent_slope):
    blocks, span_x, span_y, lanes = right_side.shape
    assert (span_x, span_y) == (2, 2)
    stresses = stress.shape[0]
    parts = stresses + 1
    steps = SWEEPS * COLOURS
    total_x, total_y = span_x * lax.axis_size("px"), span_y * lax.axis_size("py")
    vmem = pl.BlockSpec(memory_space=pltpu.VMEM)
    operands = (
        right_side.reshape(blocks * 4, lanes),
        colour.reshape(4, lanes),
        active.reshape(4, lanes),
        stress.reshape(stresses * 4, lanes),
        conduct.reshape(4, lanes),
        mass.reshape(4, lanes),
        tangent_base,
        tangent_slope,
    )
    flat = pl.pallas_call(
        functools.partial(kernel, total_x, total_y),
        out_shape=jax.ShapeDtypeStruct((blocks * 4, lanes), jnp.float32),
        in_specs=[pl.BlockSpec(memory_space=pltpu.HBM)] * 8,
        out_specs=vmem,
        scratch_shapes=[
            *[pltpu.VMEM(x.shape, x.dtype) for x in operands],
            pltpu.SemaphoreType.DMA((8,)),
            pltpu.VMEM((steps, 4, 4, blocks, lanes), jnp.float32),
            pltpu.VMEM((3, 3, stresses + 2, lanes), jnp.float32),
            pltpu.VMEM((3, 3, 2, parts, 8, lanes), jnp.float32),
            pltpu.VMEM((4, blocks, blocks, lanes), jnp.float32),
            pltpu.VMEM((blocks, 128), jnp.float32),
            pltpu.VMEM((parts, blocks, blocks, lanes), jnp.float32),
            pltpu.SemaphoreType.DMA((steps - 1, 8)),
            pltpu.SemaphoreType.DMA((steps - 1, 8)),
            pltpu.SemaphoreType.DMA((3,)),
            pltpu.SemaphoreType.DMA((3,)),
        ],
        compiler_params=pltpu.CompilerParams(
            collective_id=0, has_side_effects=True, vmem_limit_bytes=60 * 1024 * 1024
        ),
        name="gauss_seidel",
    )(*operands)
    return flat.reshape(right_side.shape)


def solution(mesh):
    return jax.shard_map(
        on_device,
        mesh=mesh,
        in_specs=(
            P(None, "px", "py", None),
            P("px", "py", None),
            P("px", "py", None),
            P(None, "px", "py", None),
            P("px", "py", None),
            P("px", "py", None),
            P(),
            P(),
        ),
        out_specs=P(None, "px", "py", None),
        check_vma=False,
    )
```

```python
import functools

import jax
import jax.numpy as jnp
from jax import lax
from jax.experimental import pallas as pl
from jax.experimental.pallas import tpu as pltpu
from jax.sharding import PartitionSpec as P

SWEEPS = 2
COLOURS = 4
SHIFT_DIAG = 0.25
MESH = pl.DeviceIdType.MESH
SIDES = [(-1, 0), (1, 0), (0, -1), (0, 1)]
CORNERS = [(-1, -1), (-1, 1), (1, -1), (1, 1)]
WAYS = CORNERS + SIDES


def kernel(
    total_x, total_y, *refs
):
    given, out_ref, staged = refs[:8], refs[8], refs[9:17]
    rhs_ref, colour_ref, active_ref, stress_ref, conduct_ref, mass_ref, base_ref, slope_ref = staged
    given_sem, field, elem, weights, inv, mat, coef, send_sem, recv_sem, elem_send, elem_recv = refs[17:]
    fetches = [pltpu.make_async_copy(a, b, given_sem.at[n]) for n, (a, b) in enumerate(zip(given, staged))]
    for fetch in fetches:
        fetch.start()
    count_x, count_y = total_x // 2, total_y // 2
    me_x, me_y = lax.axis_index("px"), lax.axis_index("py")
    lanes = rhs_ref.shape[1]
    blocks = base_ref.shape[0]
    stresses = slope_ref.shape[0]
    parts = stresses + 1

    def exists(dx, dy):
        found = None
        for delta, me, count in ((dx, me_x, count_x), (dy, me_y, count_y)):
            if delta == 0:
                continue
            one = me >= 1 if delta < 0 else me <= count - 2
            found = one if found is None else found & one
        return found

    def there(dx, dy):
        return (me_x + dx, me_y + dy)

    elem[...] = jnp.zeros_like(elem)
    field[...] = jnp.zeros_like(field)
    barrier = pltpu.get_barrier_semaphore()
    for dx, dy in WAYS:
        @pl.when(exists(dx, dy))
        def _():
            pl.semaphore_signal(barrier, inc=1, device_id=there(dx, dy), device_id_type=MESH)

    for fetch in fetches:
        fetch.wait()

    third = lax.broadcasted_iota(jnp.int32, (1, lanes), 1)
    for i in range(2):
        for j in range(2):
            c = 2 * i + j
            inside = (third < lanes - 1) & (2 * me_x + i < total_x - 1) & (2 * me_y + j < total_y - 1)
            weight = jnp.where(inside, active_ref[c : c + 1, :].astype(jnp.float32), 0.0)
            elem[1 + i, 1 + j, 0:stresses, :] = stress_ref[pl.ds(c, stresses, stride=4), :]
            elem[1 + i, 1 + j, stresses : stresses + 1, :] = weight * conduct_ref[c : c + 1, :]
            elem[1 + i, 1 + j, stresses + 1 : stresses + 2, :] = weight * mass_ref[c : c + 1, :] * 0.125

    span_x = 1 + (me_x >= 1).astype(jnp.int32) + (me_x <= count_x - 2).astype(jnp.int32)
    span_y = 1 + (me_y >= 1).astype(jnp.int32) + (me_y <= count_y - 2).astype(jnp.int32)
    pl.semaphore_wait(barrier, span_x * span_y - 1)

    def elem_copy(way, target):
        dx, dy = way
        src = (2 if dx else pl.ds(1, 2), 2 if dy else pl.ds(1, 2))
        dst = (0 if dx else pl.ds(1, 2), 0 if dy else pl.ds(1, 2))
        n = dx * 2 + dy - 1
        return pltpu.make_async_remote_copy(
            src_ref=elem.at[src[0], src[1]], dst_ref=elem.at[dst[0], dst[1]],
            send_sem=elem_send.at[n], recv_sem=elem_recv.at[n], device_id=target, device_id_type=MESH,
        )

    elem_ways = ((0, 1), (1, 0), (1, 1))
    for way in elem_ways[::-1]:
        @pl.when(exists(*way))
        def _():
            elem_copy(way, there(*way)).start()

    row = lax.broadcasted_iota(jnp.int32, (blocks, blocks), 0)
    col = lax.broadcasted_iota(jnp.int32, (blocks, blocks), 1)
    identity = jnp.where(row == col, 1.0, 0.0).astype(jnp.float32)
    mat[...] = jnp.zeros_like(mat)
    for s in range(parts):
        block = slope_ref[s] * 0.125 if s < stresses else identity + base_ref[...] * 0.125
        mat[:, s * blocks : (s + 1) * blocks] = block
        for q in range(blocks):
            coef[s, q] = jnp.broadcast_to(block[:, q : q + 1], (blocks, lanes))
    high = mat[...].astype(jnp.bfloat16)
    low = (mat[...] - high.astype(jnp.float32)).astype(jnp.bfloat16)
    left = jnp.concatenate(
        [jnp.concatenate([high, high], axis=1), jnp.concatenate([low, low], axis=1)], axis=0
    )

    line = lax.broadcasted_iota(jnp.int32, (8, lanes), 0)
    diag = {}

    def weigh(ex, ey):
        part = elem[ex, ey]
        stiff = part[stresses : stresses + 1]
        mass = part[stresses + 1 : stresses + 2]
        scaled = jnp.where(line == stresses, 1.0, part)
        diag[ex, ey] = scaled * (stiff * (1.0 / 3.0) + mass)
        off = scaled * (stiff * (1.0 / 12.0))
        for z, shown in enumerate((off, pltpu.roll(off, 1, 1))):
            for s in range(parts):
                weights[ex, ey, z, s] = jnp.broadcast_to(shown[s : s + 1], (8, lanes))

    sublane = lax.broadcasted_iota(jnp.int32, (blocks, lanes), 0)

    def assemble(i, j):
        total = diag[i, j] + diag[i + 1, j] + diag[i, j + 1] + diag[i + 1, j + 1]
        total = total + pltpu.roll(total, 1, 1)
        spread = [jnp.broadcast_to(total[s : s + 1], (blocks, lanes)) for s in range(parts)]
        for q in range(blocks):
            value = jnp.where(sublane == q, SHIFT_DIAG, 0.0)
            for s in range(parts):
                value = value + coef[s, q] * spread[s]
            inv[2 * i + j, q] = value

    def receive_elem(way):
        dx, dy = way

        @pl.when(exists(-dx, -dy))
        def _():
            elem_copy(way, there(-dx, -dy)).wait_recv()

    def invert(c, carry):
        columns = [inv[c, q] for q in range(blocks)]
        for r in range(blocks):
            factor = columns[r]
            scale = 1.0 / jnp.broadcast_to(factor[r : r + 1], (8, lanes))
            scale = jnp.concatenate([scale, scale], axis=0)
            for q in range(blocks):
                if q != r:
                    ratio = jnp.broadcast_to(columns[q][r : r + 1], (blocks, lanes)) * scale
                    columns[q] = jnp.where(sublane == r, ratio, columns[q] - factor * ratio)
            columns[r] = jnp.where(sublane == r, scale, -(factor * scale))
        for q in range(blocks):
            inv[c, q] = columns[q]
        return carry

    for ex in (1, 2):
        for ey in (1, 2):
            weigh(ex, ey)
    assemble(1, 1)
    lax.fori_loop(3, 4, invert, 0)
    receive_elem((0, 1))
    weigh(1, 0)
    weigh(2, 0)
    assemble(1, 0)
    receive_elem((1, 0))
    weigh(0, 1)
    weigh(0, 2)
    assemble(0, 1)
    lax.fori_loop(1, 3, invert, 0)
    receive_elem((1, 1))
    weigh(0, 0)
    assemble(0, 0)
    lax.fori_loop(0, 1, invert, 0)

    def solve(c, vector):
        sums = [None, None]
        for q in range(blocks):
            term = inv[c, q] * jnp.broadcast_to(vector[q : q + 1], (blocks, lanes))
            sums[q % 2] = term if sums[q % 2] is None else sums[q % 2] + term
        return sums[0] + sums[1]

    def field_copy(slot, way, target):
        n = WAYS.index(way)
        src, dst = [], []
        for delta in way:
            src.append({-1: 1, 0: pl.ds(1, 2), 1: 2}[delta])
            dst.append({-1: 3, 0: pl.ds(1, 2), 1: 0}[delta])
        return pltpu.make_async_remote_copy(
            src_ref=field.at[slot, src[0], src[1]], dst_ref=field.at[slot, dst[0], dst[1]],
            send_sem=send_sem.at[slot, n], recv_sem=recv_sem.at[slot, n], device_id=target, device_id_type=MESH,
        )

    def send(slot):
        for way in WAYS:
            @pl.when(exists(*way))
            def _():
                field_copy(slot, way, there(*way)).start()

    for i in range(2):
        for j in range(2):
            c = 2 * i + j
            first = solve(c, rhs_ref[pl.ds(c, blocks, stride=4), :])
            hit = jnp.broadcast_to(colour_ref[c : c + 1, :], (blocks, lanes)) == 0
            field[0, 1 + i, 1 + j] = jnp.where(hit, first, 0.0)
    send(0)
    for way in elem_ways:
        @pl.when(exists(*way))
        def _():
            elem_copy(way, there(*way)).wait_send()

    steps = SWEEPS * COLOURS
    gap = jnp.zeros((128 - parts * blocks, lanes), jnp.bfloat16)

    def step(t, carry):
        old, new = t - 1, t
        shade = lax.rem(t, COLOURS)
        sums = [[None] * parts for _ in range(4)]

        def receive(ways):
            for dx, dy in ways:
                @pl.when(exists(-dx, -dy))
                def _():
                    field_copy(old, (dx, dy), there(-dx, -dy)).wait_recv()

        def gather(outward):
            for c in range(4):
                i, j = c // 2, c % 2
                for dx in (-1, 1):
                    for dy in (-1, 1):
                        if (dx != 1 - 2 * i) + (dy != 1 - 2 * j) != outward:
                            continue
                        ex, ey = i + (dx > 0), j + (dy > 0)
                        corner = field[old, 1 + i + dx, 1 + j + dy]
                        cross = corner + field[old, 1 + i + dx, 1 + j] + field[old, 1 + i, 1 + j + dy]
                        for z in range(2):
                            q = corner + pltpu.roll(cross, lanes - 1 if z == 0 else 1, 1)
                            for s in range(parts):
                                w = weights[ex, ey, z, s]
                                term = jnp.concatenate([w, w], axis=0) * q
                                sums[c][s] = term if sums[c][s] is None else sums[c][s] + term

        gather(0)
        receive(SIDES)
        gather(1)
        receive(CORNERS)
        gather(2)
        fresh = []
        for i in range(2):
            pair = []
            for j in range(2):
                tops = [x.astype(jnp.bfloat16) for x in sums[2 * i + j]]
                rest = [(x - y.astype(jnp.float32)).astype(jnp.bfloat16) for x, y in zip(sums[2 * i + j], tops)]
                pair.append(jnp.concatenate([*tops, gap, *rest, gap], axis=0))
            made = jnp.dot(left, jnp.concatenate(pair, axis=1), preferred_element_type=jnp.float32)
            made = made[:blocks] + made[blocks:]
            for j in range(2):
                c = 2 * i + j
                vector = rhs_ref[pl.ds(c, blocks, stride=4), :] + made[:, j * lanes : (j + 1) * lanes]
                hit = jnp.broadcast_to(colour_ref[c : c + 1, :], (blocks, lanes)) == shade
                fresh.append(jnp.where(hit, solve(c, vector), field[old, 1 + i, 1 + j]))
        for c in range(4):
            field[new, 1 + c // 2, 1 + c % 2] = fresh[c]
        for way in WAYS:
            @pl.when(exists(*way) & (t < steps - 1))
            def _():
                field_copy(new, way, there(*way)).start()
        return carry

    lax.fori_loop(1, steps, step, 0)
    for c in range(4):
        out_ref[pl.ds(c, blocks, stride=4), :] = field[steps - 1, 1 + c // 2, 1 + c % 2]

    def finish(t, carry):
        for way in WAYS:
            @pl.when(exists(*way))
            def _():
                field_copy(t, way, there(*way)).wait_send()
        return carry

    lax.fori_loop(0, steps - 1, finish, 0)


def on_device(right_side, colour, active, stress, conduct, mass, tangent_base, tangent_slope):
    blocks, span_x, span_y, lanes = right_side.shape
    assert (span_x, span_y) == (2, 2)
    stresses = stress.shape[0]
    parts = stresses + 1
    steps = SWEEPS * COLOURS
    total_x, total_y = span_x * lax.axis_size("px"), span_y * lax.axis_size("py")
    vmem = pl.BlockSpec(memory_space=pltpu.VMEM)
    operands = (
        right_side.reshape(blocks * 4, lanes),
        colour.reshape(4, lanes),
        active.reshape(4, lanes),
        stress.reshape(stresses * 4, lanes),
        conduct.reshape(4, lanes),
        mass.reshape(4, lanes),
        tangent_base,
        tangent_slope,
    )
    flat = pl.pallas_call(
        functools.partial(kernel, total_x, total_y),
        out_shape=jax.ShapeDtypeStruct((blocks * 4, lanes), jnp.float32),
        in_specs=[pl.BlockSpec(memory_space=pltpu.HBM)] * 8,
        out_specs=vmem,
        scratch_shapes=[
            *[pltpu.VMEM(x.shape, x.dtype) for x in operands],
            pltpu.SemaphoreType.DMA((8,)),
            pltpu.VMEM((steps, 4, 4, blocks, lanes), jnp.float32),
            pltpu.VMEM((3, 3, stresses + 2, lanes), jnp.float32),
            pltpu.VMEM((3, 3, 2, parts, 8, lanes), jnp.float32),
            pltpu.VMEM((4, blocks, blocks, lanes), jnp.float32),
            pltpu.VMEM((blocks, 128), jnp.float32),
            pltpu.VMEM((parts, blocks, blocks, lanes), jnp.float32),
            pltpu.SemaphoreType.DMA((steps - 1, 8)),
            pltpu.SemaphoreType.DMA((steps - 1, 8)),
            pltpu.SemaphoreType.DMA((3,)),
            pltpu.SemaphoreType.DMA((3,)),
        ],
        compiler_params=pltpu.CompilerParams(
            collective_id=0, has_side_effects=True, vmem_limit_bytes=60 * 1024 * 1024
        ),
        name="gauss_seidel",
    )(*operands)
    return flat.reshape(right_side.shape)


def solution(mesh):
    return jax.shard_map(
        on_device,
        mesh=mesh,
        in_specs=(
            P(None, "px", "py", None),
            P("px", "py", None),
            P("px", "py", None),
            P(None, "px", "py", None),
            P("px", "py", None),
            P("px", "py", None),
            P(),
            P(),
        ),
        out_specs=P(None, "px", "py", None),
        check_vma=False,
    )
```

```python
import functools

import jax
import jax.numpy as jnp
from jax import lax
from jax.experimental import pallas as pl
from jax.experimental.pallas import tpu as pltpu
from jax.sharding import PartitionSpec as P

SWEEPS = 2
COLOURS = 4
SHIFT_DIAG = 0.25
MESH = pl.DeviceIdType.MESH
SIDES = [(-1, 0), (1, 0), (0, -1), (0, 1)]
CORNERS = [(-1, -1), (-1, 1), (1, -1), (1, 1)]
WAYS = CORNERS + SIDES


def kernel(
    total_x, total_y, *refs
):
    given, out_ref, staged = refs[:8], refs[8], refs[9:17]
    rhs_ref, colour_ref, active_ref, stress_ref, conduct_ref, mass_ref, base_ref, slope_ref = staged
    given_sem, field, elem, weights, inv, mat, coef, send_sem, recv_sem, elem_send, elem_recv = refs[17:]
    fetches = [pltpu.make_async_copy(a, b, given_sem.at[n]) for n, (a, b) in enumerate(zip(given, staged))]
    for fetch in fetches:
        fetch.start()
    count_x, count_y = total_x // 2, total_y // 2
    me_x, me_y = lax.axis_index("px"), lax.axis_index("py")
    lanes = rhs_ref.shape[1]
    blocks = base_ref.shape[0]
    stresses = slope_ref.shape[0]
    parts = stresses + 1

    def exists(dx, dy):
        found = None
        for delta, me, count in ((dx, me_x, count_x), (dy, me_y, count_y)):
            if delta == 0:
                continue
            one = me >= 1 if delta < 0 else me <= count - 2
            found = one if found is None else found & one
        return found

    def there(dx, dy):
        return (me_x + dx, me_y + dy)

    elem[...] = jnp.zeros_like(elem)
    field[...] = jnp.zeros_like(field)
    barrier = pltpu.get_barrier_semaphore()
    for dx, dy in WAYS:
        @pl.when(exists(dx, dy))
        def _():
            pl.semaphore_signal(barrier, inc=1, device_id=there(dx, dy), device_id_type=MESH)

    for fetch in fetches:
        fetch.wait()

    third = lax.broadcasted_iota(jnp.int32, (1, lanes), 1)
    for i in range(2):
        for j in range(2):
            c = 2 * i + j
            inside = (third < lanes - 1) & (2 * me_x + i < total_x - 1) & (2 * me_y + j < total_y - 1)
            weight = jnp.where(inside, active_ref[c : c + 1, :].astype(jnp.float32), 0.0)
            elem[1 + i, 1 + j, 0:stresses, :] = stress_ref[pl.ds(c, stresses, stride=4), :]
            elem[1 + i, 1 + j, stresses : stresses + 1, :] = weight * conduct_ref[c : c + 1, :]
            elem[1 + i, 1 + j, stresses + 1 : stresses + 2, :] = weight * mass_ref[c : c + 1, :] * 0.125

    span_x = 1 + (me_x >= 1).astype(jnp.int32) + (me_x <= count_x - 2).astype(jnp.int32)
    span_y = 1 + (me_y >= 1).astype(jnp.int32) + (me_y <= count_y - 2).astype(jnp.int32)
    pl.semaphore_wait(barrier, span_x * span_y - 1)

    def elem_copy(way, target):
        dx, dy = way
        src = (2 if dx else pl.ds(1, 2), 2 if dy else pl.ds(1, 2))
        dst = (0 if dx else pl.ds(1, 2), 0 if dy else pl.ds(1, 2))
        n = dx * 2 + dy - 1
        return pltpu.make_async_remote_copy(
            src_ref=elem.at[src[0], src[1]], dst_ref=elem.at[dst[0], dst[1]],
            send_sem=elem_send.at[n], recv_sem=elem_recv.at[n], device_id=target, device_id_type=MESH,
        )

    elem_ways = ((0, 1), (1, 0), (1, 1))
    for way in elem_ways[::-1]:
        @pl.when(exists(*way))
        def _():
            elem_copy(way, there(*way)).start()

    row = lax.broadcasted_iota(jnp.int32, (blocks, blocks), 0)
    col = lax.broadcasted_iota(jnp.int32, (blocks, blocks), 1)
    identity = jnp.where(row == col, 1.0, 0.0).astype(jnp.float32)
    mat[...] = jnp.zeros_like(mat)
    for s in range(parts):
        block = slope_ref[s] * 0.125 if s < stresses else identity + base_ref[...] * 0.125
        mat[:, s * blocks : (s + 1) * blocks] = block
        for q in range(blocks):
            coef[s, q] = jnp.broadcast_to(block[:, q : q + 1], (blocks, lanes))
    high = mat[...].astype(jnp.bfloat16)
    low = (mat[...] - high.astype(jnp.float32)).astype(jnp.bfloat16)
    left = jnp.concatenate(
        [jnp.concatenate([high, high], axis=1), jnp.concatenate([low, low], axis=1)], axis=0
    )

    line = lax.broadcasted_iota(jnp.int32, (8, lanes), 0)
    diag = {}

    def weigh(ex, ey):
        part = elem[ex, ey]
        stiff = part[stresses : stresses + 1]
        mass = part[stresses + 1 : stresses + 2]
        scaled = jnp.where(line == stresses, 1.0, part)
        diag[ex, ey] = scaled * (stiff * (1.0 / 3.0) + mass)
        off = scaled * (stiff * (1.0 / 12.0))
        for z, shown in enumerate((off, pltpu.roll(off, 1, 1))):
            for s in range(parts):
                weights[ex, ey, z, s] = jnp.broadcast_to(shown[s : s + 1], (8, lanes))

    sublane = lax.broadcasted_iota(jnp.int32, (blocks, lanes), 0)

    def assemble(i, j):
        total = diag[i, j] + diag[i + 1, j] + diag[i, j + 1] + diag[i + 1, j + 1]
        total = total + pltpu.roll(total, 1, 1)
        spread = [jnp.broadcast_to(total[s : s + 1], (blocks, lanes)) for s in range(parts)]
        for q in range(blocks):
            value = jnp.where(sublane == q, SHIFT_DIAG, 0.0)
            for s in range(parts):
                value = value + coef[s, q] * spread[s]
            inv[2 * i + j, q] = value

    def receive_elem(way):
        dx, dy = way

        @pl.when(exists(-dx, -dy))
        def _():
            elem_copy(way, there(-dx, -dy)).wait_recv()

    def invert(c, carry):
        columns = [inv[c, q] for q in range(blocks)]
        for r in range(blocks):
            factor = columns[r]
            scale = 1.0 / jnp.broadcast_to(factor[r : r + 1], (8, lanes))
            scale = jnp.concatenate([scale, scale], axis=0)
            for q in range(blocks):
                if q != r:
                    ratio = jnp.broadcast_to(columns[q][r : r + 1], (blocks, lanes)) * scale
                    columns[q] = jnp.where(sublane == r, ratio, columns[q] - factor * ratio)
            columns[r] = jnp.where(sublane == r, scale, -(factor * scale))
        for q in range(blocks):
            inv[c, q] = columns[q]
        return carry

    for ex in (1, 2):
        for ey in (1, 2):
            weigh(ex, ey)
    assemble(1, 1)
    lax.fori_loop(3, 4, invert, 0)
    receive_elem((0, 1))
    weigh(1, 0)
    weigh(2, 0)
    assemble(1, 0)
    receive_elem((1, 0))
    weigh(0, 1)
    weigh(0, 2)
    assemble(0, 1)
    lax.fori_loop(1, 3, invert, 0)
    receive_elem((1, 1))
    weigh(0, 0)
    assemble(0, 0)
    lax.fori_loop(0, 1, invert, 0)

    def solve(c, vector):
        sums = [None, None]
        for q in range(blocks):
            term = inv[c, q] * jnp.broadcast_to(vector[q : q + 1], (blocks, lanes))
            sums[q % 2] = term if sums[q % 2] is None else sums[q % 2] + term
        return sums[0] + sums[1]

    def field_copy(slot, way, target):
        n = WAYS.index(way)
        src, dst = [], []
        for delta in way:
            src.append({-1: 1, 0: pl.ds(1, 2), 1: 2}[delta])
            dst.append({-1: 3, 0: pl.ds(1, 2), 1: 0}[delta])
        return pltpu.make_async_remote_copy(
            src_ref=field.at[slot, src[0], src[1]], dst_ref=field.at[slot, dst[0], dst[1]],
            send_sem=send_sem.at[slot, n], recv_sem=recv_sem.at[slot, n], device_id=target, device_id_type=MESH,
        )

    def send(slot):
        for way in WAYS:
            @pl.when(exists(*way))
            def _():
                field_copy(slot, way, there(*way)).start()

    for i in range(2):
        for j in range(2):
            c = 2 * i + j
            first = solve(c, rhs_ref[pl.ds(c, blocks, stride=4), :])
            hit = jnp.broadcast_to(colour_ref[c : c + 1, :], (blocks, lanes)) == 0
            field[0, 1 + i, 1 + j] = jnp.where(hit, first, 0.0)
    send(0)
    for way in elem_ways:
        @pl.when(exists(*way))
        def _():
            elem_copy(way, there(*way)).wait_send()

    steps = SWEEPS * COLOURS
    gap = jnp.zeros((128 - parts * blocks, lanes), jnp.bfloat16)

    def step(t, carry):
        old, new = t - 1, t
        shade = lax.rem(t, COLOURS)
        sums = [[None] * parts for _ in range(4)]

        def receive(ways):
            for dx, dy in ways:
                @pl.when(exists(-dx, -dy))
                def _():
                    field_copy(old, (dx, dy), there(-dx, -dy)).wait_recv()

        def gather(outward):
            for c in range(4):
                i, j = c // 2, c % 2
                for dx in (-1, 1):
                    for dy in (-1, 1):
                        if (dx != 1 - 2 * i) + (dy != 1 - 2 * j) != outward:
                            continue
                        ex, ey = i + (dx > 0), j + (dy > 0)
                        corner = field[old, 1 + i + dx, 1 + j + dy]
                        cross = corner + field[old, 1 + i + dx, 1 + j] + field[old, 1 + i, 1 + j + dy]
                        for z in range(2):
                            q = corner + pltpu.roll(cross, lanes - 1 if z == 0 else 1, 1)
                            for s in range(parts):
                                w = weights[ex, ey, z, s]
                                term = jnp.concatenate([w, w], axis=0) * q
                                sums[c][s] = term if sums[c][s] is None else sums[c][s] + term

        gather(0)
        receive(SIDES)
        gather(1)
        receive(CORNERS)
        gather(2)
        for i in range(2):
            pair = []
            for j in range(2):
                tops = [x.astype(jnp.bfloat16) for x in sums[2 * i + j]]
                rest = [(x - y.astype(jnp.float32)).astype(jnp.bfloat16) for x, y in zip(sums[2 * i + j], tops)]
                pair.append(jnp.concatenate([*tops, gap, *rest, gap], axis=0))
            made = jnp.dot(left, jnp.concatenate(pair, axis=1), preferred_element_type=jnp.float32)
            made = made[:blocks] + made[blocks:]
            for j in range(2):
                c = 2 * i + j
                vector = rhs_ref[pl.ds(c, blocks, stride=4), :] + made[:, j * lanes : (j + 1) * lanes]
                hit = jnp.broadcast_to(colour_ref[c : c + 1, :], (blocks, lanes)) == shade
                field[new, 1 + i, 1 + j] = jnp.where(hit, solve(c, vector), field[old, 1 + i, 1 + j])
            for way in WAYS:
                if (way[0] == -1) != (i == 0):
                    continue

                @pl.when(exists(*way) & (t < steps - 1))
                def _():
                    field_copy(new, way, there(*way)).start()
        return carry

    lax.fori_loop(1, steps, step, 0)
    for c in range(4):
        out_ref[pl.ds(c, blocks, stride=4), :] = field[steps - 1, 1 + c // 2, 1 + c % 2]

    def finish(t, carry):
        for way in WAYS:
            @pl.when(exists(*way))
            def _():
                field_copy(t, way, there(*way)).wait_send()
        return carry

    lax.fori_loop(0, steps - 1, finish, 0)


def on_device(right_side, colour, active, stress, conduct, mass, tangent_base, tangent_slope):
    blocks, span_x, span_y, lanes = right_side.shape
    assert (span_x, span_y) == (2, 2)
    stresses = stress.shape[0]
    parts = stresses + 1
    steps = SWEEPS * COLOURS
    total_x, total_y = span_x * lax.axis_size("px"), span_y * lax.axis_size("py")
    vmem = pl.BlockSpec(memory_space=pltpu.VMEM)
    operands = (
        right_side.reshape(blocks * 4, lanes),
        colour.reshape(4, lanes),
        active.reshape(4, lanes),
        stress.reshape(stresses * 4, lanes),
        conduct.reshape(4, lanes),
        mass.reshape(4, lanes),
        tangent_base,
        tangent_slope,
    )
    flat = pl.pallas_call(
        functools.partial(kernel, total_x, total_y),
        out_shape=jax.ShapeDtypeStruct((blocks * 4, lanes), jnp.float32),
        in_specs=[pl.BlockSpec(memory_space=pltpu.HBM)] * 8,
        out_specs=vmem,
        scratch_shapes=[
            *[pltpu.VMEM(x.shape, x.dtype) for x in operands],
            pltpu.SemaphoreType.DMA((8,)),
            pltpu.VMEM((steps, 4, 4, blocks, lanes), jnp.float32),
            pltpu.VMEM((3, 3, stresses + 2, lanes), jnp.float32),
            pltpu.VMEM((3, 3, 2, parts, 8, lanes), jnp.float32),
            pltpu.VMEM((4, blocks, blocks, lanes), jnp.float32),
            pltpu.VMEM((blocks, 128), jnp.float32),
            pltpu.VMEM((parts, blocks, blocks, lanes), jnp.float32),
            pltpu.SemaphoreType.DMA((steps - 1, 8)),
            pltpu.SemaphoreType.DMA((steps - 1, 8)),
            pltpu.SemaphoreType.DMA((3,)),
            pltpu.SemaphoreType.DMA((3,)),
        ],
        compiler_params=pltpu.CompilerParams(
            collective_id=0, has_side_effects=True, vmem_limit_bytes=60 * 1024 * 1024
        ),
        name="gauss_seidel",
    )(*operands)
    return flat.reshape(right_side.shape)


def solution(mesh):
    return jax.shard_map(
        on_device,
        mesh=mesh,
        in_specs=(
            P(None, "px", "py", None),
            P("px", "py", None),
            P("px", "py", None),
            P(None, "px", "py", None),
            P("px", "py", None),
            P("px", "py", None),
            P(),
            P(),
        ),
        out_specs=P(None, "px", "py", None),
        check_vma=False,
    )
```
